256 devices in a mesh: snp: 16 (over x, y_hi, core), samp: 16 (over z, y_lo).
Axes of the slice: x: 4, y: 4 (y_hi: 2, y_lo: 2; y = y_hi * 2 + y_lo), z: 8, core: 2. Of those that a mesh axis runs over, the one named last changes fastest.
Arguments:
- dosage: int32 [16384, 16384], P('samp', 'snp'), may hold values from -1 to 2, as said below
Outputs:
- ld_band: float32 [16384, 3, 1024], P(('snp', 'samp'))
The draws below stay inside these ranges and needn't reach their ends.
Inputs may be any that keep to these rules, and one draw needn't show every extreme that they name: `dosage`: neighbouring SNPs are correlated; each SNP's allele frequency lies between 5 and 95 percent.
All inputs are finite; a program needn't handle non-finite values.
Results may differ from the reference program's by a relative error of at most 0.003.
The reference program's roundings to bfloat16 on the way (of `standard`) count: a program that leaves them out, or rounds other values in their place, can miss the bound.
Values may be sent and summed in bfloat16 or wider, within the bound.
A program may use at most 64 MiB of HBM per device.

```python
import jax
import jax.numpy as jnp
from jax import lax

B = 1024
PERSONS = 16384
NSNP = 16384


def draw_dosage(key, part):
    key = jax.random.fold_in(key, 7)
    freq = jax.random.randint(jax.random.fold_in(key, 1), (NSNP,), 5, 96)
    first = (jax.random.randint(jax.random.fold_in(key, 2), (2, PERSONS), 0, 100) < freq[0]).astype(jnp.int32)

    def advance(carry, position):
        step_key = jax.random.fold_in(key, position + 10)
        fresh = (jax.random.randint(jax.random.fold_in(step_key, 0), (2, PERSONS), 0, 100) < freq[position]).astype(jnp.int32)
        keep = jax.random.randint(jax.random.fold_in(step_key, 1), (2, PERSONS), 0, 4) != 0
        allele = jnp.where(keep, carry, fresh)
        return (allele, allele[0] + allele[1])
    last, rest = lax.scan(advance, first, jnp.arange(1, NSNP, dtype=jnp.int32))
    head = (first[0] + first[1])[None, :]
    counts = jnp.concatenate([head, rest], axis=0).T.astype(jnp.int32)
    called = jax.random.randint(jax.random.fold_in(key, 3), (PERSONS, NSNP), 0, 10) < 9
    return jnp.where(called, counts, -1).astype(jnp.int32)


def setup_inputs(seed: int = 0) -> dict:
    seeds = jax.random.split(jax.random.key(seed), 2)
    dosage = draw_dosage(jax.random.fold_in(seeds[1], 71), 0)
    return dict(dosage=dosage)


def reference(dosage):
    called = (dosage >= 0).astype(jnp.float32)
    geno = jnp.maximum(dosage, 0).astype(jnp.float32)
    count = lax.optimization_barrier(jnp.sum(called, axis=0))
    total = lax.optimization_barrier(jnp.sum(called * geno, axis=0))
    safe = jnp.maximum(count, 1.0)
    mean = total / safe
    deviation = called * (geno - mean)
    centred = lax.optimization_barrier(jnp.sum(deviation * deviation, axis=0))
    spread = 1.0 / jnp.sqrt(centred / safe + 1e-05)
    standard = (deviation * spread).astype(jnp.bfloat16)
    padded = jnp.concatenate([standard, jnp.zeros((standard.shape[0], 2 * B), jnp.bfloat16)], axis=1)
    nblocks = standard.shape[1] // B

    def one_block(index):
        start = (index * B).astype(jnp.int32)
        window = lax.dynamic_slice_in_dim(padded, start, 3 * B, 1).astype(jnp.float32)
        own = window[:, :B]
        others = window.reshape(window.shape[0], 3, B)
        return jnp.einsum('pr,pjc->rjc', own, others) / float(PERSONS)
    tiles = lax.map(one_block, jnp.arange(nblocks, dtype=jnp.int32))
    return tiles.reshape(nblocks * B, 3, B)
```

```python
import functools

import jax
import jax.numpy as jnp
from jax import lax
from jax.experimental import pallas as pl
from jax.experimental.pallas import tpu as pltpu
from jax.sharding import PartitionSpec as P

MESH = pl.DeviceIdType.MESH
F32 = jnp.float32
BF16 = jnp.bfloat16

W = 256
Q = 4
G = 6
ZR = 128
YR = 64


def kernel(
    nsnp, nsamp, dosage, out,
    held, raw, cols, own_t, stat_own, stat_in, ms_own, ms_in,
    part, sent, got, ysent, ygot, mine,
    load_sem, stat_s, stat_r, ms_s, ms_r, ahead_s, ahead_r, sib_s, sib_r, sent_s, got_r, ys_s, ys_r,
):
    people, width = held.shape
    persons = float(people * nsamp)
    snp = lax.axis_index("snp")
    samp = lax.axis_index("samp")
    odd = lax.rem(snp, 2)
    ylo = lax.rem(samp, 2)
    z = samp // 2
    nz = nsamp // 2
    behind = (lax.rem(snp + nsnp - 2, nsnp), samp)
    front = (lax.rem(snp + 2, nsnp), samp)
    sibling = (snp + 1 - 2 * odd, samp)
    pair = (snp, samp + 1 - 2 * ylo)
    ring = ((snp, lax.rem(samp + 2, nsamp)), (snp, lax.rem(samp + nsamp - 2, nsamp)))

    barrier = pltpu.get_barrier_semaphore()
    for d in (behind, front, sibling):
        pl.semaphore_signal(barrier, inc=1, device_id=d, device_id_type=MESH)

    def greet(o, _):
        pl.semaphore_signal(
            barrier, inc=1, device_id=(snp, lax.rem(samp + o, nsamp)), device_id_type=MESH
        )
        return 0

    lax.fori_loop(1, nsamp, greet, 0)

    parts = 4
    step = people // parts

    def load(i):
        rows = pl.ds(i * step, step)
        return pltpu.make_async_copy(dosage.at[rows], held.at[rows], load_sem.at[i])

    for i in range(parts):
        load(i).start()

    def slab(i, acc):
        s1, s2, sm = acc
        x = held[pl.ds(pl.multiple_of(i * 16, 16), 16), :].astype(F32)
        xb = x.astype(BF16)
        for q in range(Q):
            raw[q, pl.ds(pl.multiple_of(i * 16, 16), 16), :] = xb[:, q * W : (q + 1) * W]
        lo, hi = x[:8], x[8:]
        s1 = s1 + (lo + hi)
        s2 = s2 + (lo * lo + hi * hi)
        sm = sm + (jnp.minimum(lo, 0.0) + jnp.minimum(hi, 0.0))
        return s1, s2, sm

    zero = jnp.zeros((8, width), F32)
    acc = (zero, zero, zero)
    for i in range(parts):
        load(i).wait()
        acc = lax.fori_loop(i * (step // 16), (i + 1) * (step // 16), slab, acc)
    for n, a in enumerate(acc):
        row = jnp.sum(a, axis=0, keepdims=True)
        for b in range(8):
            stat_own[n * 8 + b : n * 8 + b + 1, :] = row[:, b * 128 : (b + 1) * 128]

    pl.semaphore_wait(barrier, nsamp - 1 + 3)

    def stat_copy(o):
        return pltpu.make_async_remote_copy(
            src_ref=stat_own, dst_ref=stat_in.at[samp],
            send_sem=stat_s.at[o], recv_sem=stat_r.at[samp],
            device_id=(snp, lax.rem(samp + o, nsamp)), device_id_type=MESH,
        )

    def stat_start(o, _):
        stat_copy(o).start()
        return 0

    lax.fori_loop(1, nsamp, stat_start, 0)

    def ahead_copy(q):
        return pltpu.make_async_remote_copy(
            src_ref=raw.at[q], dst_ref=cols.at[2 * Q + q],
            send_sem=ahead_s.at[q], recv_sem=ahead_r.at[q],
            device_id=behind, device_id_type=MESH,
        )

    for q in range(Q):
        ahead_copy(q).start()

    def stat_take(o, acc):
        src = lax.rem(samp + o, nsamp)
        pltpu.make_async_remote_copy(
            src_ref=stat_own, dst_ref=stat_in.at[src],
            send_sem=stat_s.at[o], recv_sem=stat_r.at[src],
            device_id=(snp, src), device_id_type=MESH,
        ).wait_recv()
        return acc + stat_in[src]

    sums = lax.fori_loop(1, nsamp, stat_take, stat_own[...])
    missing = -sums[16:24]
    count = persons - missing
    total = sums[0:8] + missing
    square = sums[8:16] - missing
    safe = jnp.maximum(count, 1.0)
    ci, ti, si = count.astype(jnp.int32), total.astype(jnp.int32), square.astype(jnp.int32)
    spare = (ci * si - ti * ti).astype(F32)
    ms_own[0:8, :] = total / safe
    ms_own[8:16, :] = 1.0 / jnp.sqrt(spare / (safe * safe) + 1e-05)

    def ms_copy():
        return pltpu.make_async_remote_copy(
            src_ref=ms_own, dst_ref=ms_in, send_sem=ms_s, recv_sem=ms_r,
            device_id=behind, device_id_type=MESH,
        )

    ms_copy().start()

    def row_of(ref, base, q):
        return jnp.concatenate([ref[base + 2 * q : base + 2 * q + 1, :], ref[base + 2 * q + 1 : base + 2 * q + 2, :]], axis=1)

    def standardise(src, sq, dq, ref, q, keep, turned):
        mean = row_of(ref, 0, q)
        spread = row_of(ref, 8, q) * keep

        def body(i, _):
            rows = pl.ds(pl.multiple_of(i * 128, 128), 128)
            v = src[sq, rows, :].astype(F32)
            s = jnp.where(v >= 0, (v - mean) * spread, 0.0).astype(BF16)
            cols[dq, rows, :] = s
            if turned:
                own_t[pl.ds(q * W, W), rows] = s.T
            return 0

        lax.fori_loop(0, people // 128, body, 0)

    def sib_copy(src_chunk, q):
        return pltpu.make_async_remote_copy(
            src_ref=cols.at[src_chunk], dst_ref=cols.at[Q + q],
            send_sem=sib_s.at[q], recv_sem=sib_r.at[q],
            device_id=sibling, device_id_type=MESH,
        )

    for q in range(Q):
        standardise(raw, q, q, ms_own, q, 1.0, True)

        @pl.when(odd == 1)
        def _():
            sib_copy(q, q).start()

    keep = jnp.where(snp + 2 < nsnp, 1.0, 0.0)

    def take_ahead(half):
        for q in (2 * half, 2 * half + 1):
            ahead_copy(q).wait_recv()
            if q == 0:
                ms_copy().wait_recv()
            standardise(cols, 2 * Q + q, 2 * Q + q, ms_in, q, keep, False)

            @pl.when(odd == 0)
            def _():
                sib_copy(2 * Q + q, q).start()

    def take_sibling(half):
        for q in (2 * half, 2 * half + 1):
            sib_copy(q, q).wait_recv()

    def first_chunk(g):
        late = jnp.maximum(g - 2, 0)
        turned = 2 * (2 - late % 2) + late // 2
        at = jnp.where(jnp.logical_and(odd == 1, g >= 2), turned, g)
        return 2 * at

    def product(distance, chunk):
        rows = pl.multiple_of(lax.rem(z + nz + distance, nz) * ZR, ZR)
        return jnp.dot(own_t[pl.ds(rows, ZR), :], cols[chunk], preferred_element_type=F32)

    def half_copy(g, way):
        return pltpu.make_async_remote_copy(
            src_ref=sent.at[g, way, 0, way], dst_ref=got.at[g, way, 0, way],
            send_sem=sent_s.at[g, way, 0], recv_sem=got_r.at[g, way, 0],
            device_id=ring[way], device_id_type=MESH,
        )

    def full_copy(g, way, t):
        return pltpu.make_async_remote_copy(
            src_ref=sent.at[g, way, t], dst_ref=got.at[g, way, t],
            send_sem=sent_s.at[g, way, t], recv_sem=got_r.at[g, way, t],
            device_id=ring[way], device_id_type=MESH,
        )

    def chain(g, t):
        chunk = first_chunk(g)
        if t == 0:
            for way in range(2):
                sent[g, way, 0, way] = product(4, chunk + way).astype(BF16)
                half_copy(g, way).start()
            return
        for way in range(2):
            distance = (4 - t) * (1 - 2 * way)
            for h in range(2):
                part[way, h] = product(distance, chunk + h)
        for way in range(2):
            if t == 1:
                half_copy(g, way).wait_recv()
            else:
                full_copy(g, way, t - 1).wait_recv()
            for h in range(2):
                p = part[way, h]
                if t > 1 or h == way:
                    p = p + got[g, way, t - 1, h].astype(F32)
                sent[g, way, t, h] = p.astype(BF16)
            full_copy(g, way, t).start()

    def pair_copy(g):
        return pltpu.make_async_remote_copy(
            src_ref=ysent.at[g], dst_ref=ygot.at[g],
            send_sem=ys_s.at[g], recv_sem=ys_r.at[g],
            device_id=pair, device_id_type=MESH,
        )

    def finish(g):
        chunk = first_chunk(g)
        for h in range(2):
            part[0, h] = product(0, chunk + h)
        for way in range(2):
            full_copy(g, way, 3).wait_recv()
        for h in range(2):
            part[0, h] = part[0, h] + got[g, 0, 3, h].astype(F32) + got[g, 1, 3, h].astype(F32)
        other = pl.multiple_of((1 - ylo) * YR, YR)
        own = pl.multiple_of(ylo * YR, YR)
        for h in range(2):
            ysent[g, h] = part[0, h, pl.ds(other, YR), :].astype(BF16)
            mine[g, h] = part[0, h, pl.ds(own, YR), :]
        pair_copy(g).start()

    def settle(g):
        chunk = first_chunk(g)
        pair_copy(g).wait_recv()
        for h in range(2):
            c = chunk + h
            lanes = pl.ds(pl.multiple_of(lax.rem(c, Q) * W, W), W)
            out[c // Q, :, lanes] = (mine[g, h] + ygot[g, h].astype(F32)) * (1.0 / persons)

    def body(g, _):
        @pl.when(jnp.logical_and(odd == 0, g == 2))
        def _():
            take_sibling(0)

        @pl.when(jnp.logical_and(odd == 0, g == 3))
        def _():
            take_sibling(1)

        @pl.when(jnp.logical_or(jnp.logical_and(odd == 0, g == 4), jnp.logical_and(odd == 1, g == 2)))
        def _():
            take_ahead(0)

        @pl.when(jnp.logical_or(jnp.logical_and(odd == 0, g == 5), jnp.logical_and(odd == 1, g == 4)))
        def _():
            take_ahead(1)

        @pl.when(jnp.logical_and(odd == 1, g == 3))
        def _():
            take_sibling(0)

        @pl.when(jnp.logical_and(odd == 1, g == 5))
        def _():
            take_sibling(1)

        @pl.when(g < G)
        def _():
            chain(g, 0)

        @pl.when(jnp.logical_and(g >= 1, g <= G))
        def _():
            chain(g - 1, 2)

        @pl.when(jnp.logical_and(g >= 2, g <= G + 1))
        def _():
            finish(g - 2)

        @pl.when(g < G)
        def _():
            chain(g, 1)

        @pl.when(jnp.logical_and(g >= 1, g <= G))
        def _():
            chain(g - 1, 3)

        @pl.when(g >= 3)
        def _():
            settle(g - 3)

        return 0

    lax.fori_loop(0, G + 3, body, 0)

    def stat_left(o, _):
        stat_copy(o).wait_send()
        return 0

    lax.fori_loop(1, nsamp, stat_left, 0)
    ms_copy().wait_send()
    for q in range(Q):
        ahead_copy(q).wait_send()
        sib_copy(q, q).wait_send()

    def left(g, _):
        for way in range(2):
            half_copy(g, way).wait_send()
            for t in range(1, 4):
                full_copy(g, way, t).wait_send()
        pair_copy(g).wait_send()
        return 0

    lax.fori_loop(0, G, left, 0)


def per_device(dosage):
    people, width = dosage.shape
    nsnp, nsamp = lax.axis_size("snp"), lax.axis_size("samp")
    dma = pltpu.SemaphoreType.DMA
    tiles = pl.pallas_call(
        functools.partial(kernel, nsnp, nsamp),
        out_shape=jax.ShapeDtypeStruct((3, YR, width), F32),
        in_specs=[pl.BlockSpec(memory_space=pl.ANY)],
        out_specs=pl.BlockSpec(memory_space=pltpu.VMEM),
        scratch_shapes=[
            pltpu.VMEM((people, width), jnp.int32),
            pltpu.VMEM((Q, people, W), BF16),
            pltpu.VMEM((3 * Q, people, W), BF16),
            pltpu.VMEM((width, people), BF16),
            pltpu.VMEM((24, 128), F32),
            pltpu.VMEM((nsamp, 24, 128), F32),
            pltpu.VMEM((16, 128), F32),
            pltpu.VMEM((16, 128), F32),
            pltpu.VMEM((2, 2, ZR, W), F32),
            pltpu.VMEM((G, 2, 4, 2, ZR, W), BF16),
            pltpu.VMEM((G, 2, 4, 2, ZR, W), BF16),
            pltpu.VMEM((G, 2, YR, W), BF16),
            pltpu.VMEM((G, 2, YR, W), BF16),
            pltpu.VMEM((G, 2, YR, W), F32),
            dma((4,)),
            dma((nsamp,)),
            dma((nsamp,)),
            dma,
            dma,
            dma((Q,)),
            dma((Q,)),
            dma((Q,)),
            dma((Q,)),
            dma((G, 2, 4)),
            dma((G, 2, 4)),
            dma((G,)),
            dma((G,)),
        ],
        compiler_params=pltpu.CompilerParams(
            collective_id=0, has_side_effects=True, vmem_limit_bytes=56 * 2**20
        ),
        name="ld_band",
    )(dosage)
    return jnp.transpose(tiles, (1, 0, 2))


def solution(mesh):
    in_specs = (P("samp", "snp"),)
    out_specs = P(("snp", "samp"), None, None)
    return jax.shard_map(
        per_device, mesh=mesh, in_specs=in_specs, out_specs=out_specs, check_vma=False
    )
```

```python
import functools

import jax
import jax.numpy as jnp
from jax import lax
from jax.experimental import pallas as pl
from jax.experimental.pallas import tpu as pltpu
from jax.sharding import PartitionSpec as P

MESH = pl.DeviceIdType.MESH
F32 = jnp.float32
BF16 = jnp.bfloat16

W = 256
Q = 4
H = 128
YR = 64
FAR = 2 * Q
G = 3 + FAR
ODD_ORDER = (8, 4, 9, 5, 10, 6, 11, 7)


def pick(i, values):
    out = values[0]
    for n in range(1, len(values)):
        out = jnp.where(i == n, values[n], out)
    return out


def kernel(
    nsnp, nsamp, dosage, out,
    held, raw, cols, own_t, stat_own, stat_in, ms_own, ms_in,
    sent, got, last_sent, last_got,
    diag_mine, diag_ys, diag_yg, last_mine, last_ys, last_yg, far_mine, far_ys, far_yg, mirror, mirrored, turn,
    load_sem, stat_s, stat_r, ms_s, ms_r, ahead_s, ahead_r, sib_s, sib_r, sent_s, got_r, ys_s, ys_r, mir_s, mir_r,
):
    people, width = held.shape
    persons = float(people * nsamp)
    snp = lax.axis_index("snp")
    samp = lax.axis_index("samp")
    odd = lax.rem(snp, 2)
    ylo = lax.rem(samp, 2)
    z = samp // 2
    nz = nsamp // 2
    behind = (lax.rem(snp + nsnp - 2, nsnp), samp)
    front = (lax.rem(snp + 2, nsnp), samp)
    sibling = (snp + 1 - 2 * odd, samp)
    pair = (snp, samp + 1 - 2 * ylo)
    ring = ((snp, lax.rem(samp + 2, nsamp)), (snp, lax.rem(samp + nsamp - 2, nsamp)))

    barrier = pltpu.get_barrier_semaphore()
    for d in (behind, front, sibling):
        pl.semaphore_signal(barrier, inc=1, device_id=d, device_id_type=MESH)

    def greet(o, _):
        pl.semaphore_signal(
            barrier, inc=1, device_id=(snp, lax.rem(samp + o, nsamp)), device_id_type=MESH
        )
        return 0

    lax.fori_loop(1, nsamp, greet, 0)

    parts = 4
    step = people // parts

    def load(i):
        rows = pl.ds(i * step, step)
        return pltpu.make_async_copy(dosage.at[rows], held.at[rows], load_sem.at[i])

    for i in range(parts):
        load(i).start()

    def slab(i, acc):
        s1, s2, sm = acc
        x = held[pl.ds(pl.multiple_of(i * 16, 16), 16), :].astype(F32)
        xb = x.astype(BF16)
        for q in range(Q):
            raw[q, pl.ds(pl.multiple_of(i * 16, 16), 16), :] = xb[:, q * W : (q + 1) * W]
        lo, hi = x[:8], x[8:]
        s1 = s1 + (lo + hi)
        s2 = s2 + (lo * lo + hi * hi)
        sm = sm + (jnp.minimum(lo, 0.0) + jnp.minimum(hi, 0.0))
        return s1, s2, sm

    zero = jnp.zeros((8, width), F32)
    acc = (zero, zero, zero)
    for i in range(parts):
        load(i).wait()
        acc = lax.fori_loop(i * (step // 16), (i + 1) * (step // 16), slab, acc)
    for n, a in enumerate(acc):
        row = jnp.sum(a, axis=0, keepdims=True)
        for b in range(8):
            stat_own[n * 8 + b : n * 8 + b + 1, :] = row[:, b * 128 : (b + 1) * 128]

    pl.semaphore_wait(barrier, nsamp - 1 + 3)

    def stat_copy(o):
        return pltpu.make_async_remote_copy(
            src_ref=stat_own, dst_ref=stat_in.at[samp],
            send_sem=stat_s.at[o], recv_sem=stat_r.at[samp],
            device_id=(snp, lax.rem(samp + o, nsamp)), device_id_type=MESH,
        )

    def stat_start(o, _):
        stat_copy(o).start()
        return 0

    lax.fori_loop(1, nsamp, stat_start, 0)

    def ahead_copy(q):
        return pltpu.make_async_remote_copy(
            src_ref=raw.at[q], dst_ref=cols.at[2 * Q + q],
            send_sem=ahead_s.at[q], recv_sem=ahead_r.at[q],
            device_id=behind, device_id_type=MESH,
        )

    def stat_take(o, acc):
        src = lax.rem(samp + o, nsamp)
        pltpu.make_async_remote_copy(
            src_ref=stat_own, dst_ref=stat_in.at[src],
            send_sem=stat_s.at[o], recv_sem=stat_r.at[src],
            device_id=(snp, src), device_id_type=MESH,
        ).wait_recv()
        return acc + stat_in[src]

    sums = lax.fori_loop(1, nsamp, stat_take, stat_own[...])
    missing = -sums[16:24]
    count = persons - missing
    total = sums[0:8] + missing
    square = sums[8:16] - missing
    safe = jnp.maximum(count, 1.0)
    ci, ti, si = count.astype(jnp.int32), total.astype(jnp.int32), square.astype(jnp.int32)
    spare = (ci * si - ti * ti).astype(F32)
    ms_own[0:8, :] = total / safe
    ms_own[8:16, :] = 1.0 / jnp.sqrt(spare / (safe * safe) + 1e-05)

    def ms_copy():
        return pltpu.make_async_remote_copy(
            src_ref=ms_own, dst_ref=ms_in, send_sem=ms_s, recv_sem=ms_r,
            device_id=behind, device_id_type=MESH,
        )

    ms_copy().start()
    for q in range(Q):
        ahead_copy(q).start()

    def row_of(ref, base, q):
        return jnp.concatenate([ref[base + 2 * q : base + 2 * q + 1, :], ref[base + 2 * q + 1 : base + 2 * q + 2, :]], axis=1)

    def standardise(src, sq, dq, ref, q, keep, turned):
        mean = row_of(ref, 0, q)
        spread = row_of(ref, 8, q) * keep

        def body(i, _):
            rows = pl.ds(pl.multiple_of(i * 128, 128), 128)
            v = src[sq, rows, :].astype(F32)
            s = jnp.where(v >= 0, (v - mean) * spread, 0.0).astype(BF16)
            cols[dq, rows, :] = s
            if turned:
                own_t[pl.ds(q * W, W), rows] = s.T
            return 0

        lax.fori_loop(0, people // 128, body, 0)

    def sib_copy(src_chunk, q):
        return pltpu.make_async_remote_copy(
            src_ref=cols.at[src_chunk], dst_ref=cols.at[Q + q],
            send_sem=sib_s.at[q], recv_sem=sib_r.at[q],
            device_id=sibling, device_id_type=MESH,
        )

    for q in range(Q):
        standardise(raw, q, q, ms_own, q, 1.0, True)

        @pl.when(odd == 1)
        def _():
            sib_copy(q, q).start()

    keep = jnp.where(snp + 2 < nsnp, 1.0, 0.0)

    def take_ahead(q):
        ahead_copy(q).wait_recv()
        if q == 0:
            ms_copy().wait_recv()
        standardise(cols, 2 * Q + q, 2 * Q + q, ms_in, q, keep, False)

        @pl.when(odd == 0)
        def _():
            sib_copy(2 * Q + q, q).start()

    def far_chunk(g):
        return jnp.where(odd == 1, pick(g - 3, ODD_ORDER), g + 1)

    def piece(at, offset):
        c = lax.rem(at + offset, nz)
        return cols[c // 2, :, pl.ds(pl.multiple_of(lax.rem(c, 2) * H, H), H)]

    def product(kind, g, distance):
        at = lax.rem(z + nz + distance, nz)
        left = own_t[pl.ds(pl.multiple_of(at * H, H), H), :]

        def dot(right):
            return jnp.dot(left, right, preferred_element_type=F32)

        if kind == "far":
            return dot(cols[far_chunk(g)])
        if kind == "last":
            return dot(piece(at, 4))
        return jnp.concatenate([dot(piece(at, 6 * g)), dot(piece(at, 1 + 2 * g))], axis=1)

    def buffers(kind, g):
        if kind == "last":
            return last_sent, last_got
        slot = g if kind == "diag" else g - 1
        return sent.at[slot], got.at[slot]

    def half_copy(kind, g, way):
        s, r = buffers(kind, g)
        rows = pl.ds(way * YR, YR)
        return pltpu.make_async_remote_copy(
            src_ref=s.at[way, 0, rows], dst_ref=r.at[way, 0, rows],
            send_sem=sent_s.at[g, way, 0], recv_sem=got_r.at[g, way, 0],
            device_id=ring[way], device_id_type=MESH,
        )

    def full_copy(kind, g, way, t):
        s, r = buffers(kind, g)
        return pltpu.make_async_remote_copy(
            src_ref=s.at[way, t], dst_ref=r.at[way, t],
            send_sem=sent_s.at[g, way, t], recv_sem=got_r.at[g, way, t],
            device_id=ring[way], device_id_type=MESH,
        )

    def chain(kind, g, t):
        s, r = buffers(kind, g)
        if t == 0:
            p = product(kind, g, 4).astype(BF16)
            for way in range(2):
                s[way, 0, way * YR : (way + 1) * YR, :] = p[way * YR : (way + 1) * YR]
                half_copy(kind, g, way).start()
            return
        for way in range(2):
            p = product(kind, g, (4 - t) * (1 - 2 * way))
            if t == 1:
                half_copy(kind, g, way).wait_recv()
                for h in range(2):
                    rows = slice(h * YR, (h + 1) * YR)
                    ph = p[rows]
                    if h == way:
                        ph = ph + r[way, 0, rows, :].astype(F32)
                    s[way, 1, rows, :] = ph.astype(BF16)
            else:
                full_copy(kind, g, way, t - 1).wait_recv()
                s[way, t] = (p + r[way, t - 1].astype(F32)).astype(BF16)
            full_copy(kind, g, way, t).start()

    def pair_copy(kind, g):
        if kind == "diag":
            src, dst = diag_ys.at[g], diag_yg.at[g]
        elif kind == "last":
            src, dst = last_ys, last_yg
        else:
            src, dst = far_ys.at[g - 3], far_yg.at[g - 3]
        return pltpu.make_async_remote_copy(
            src_ref=src, dst_ref=dst, send_sem=ys_s.at[g], recv_sem=ys_r.at[g],
            device_id=pair, device_id_type=MESH,
        )

    other_rows = pl.ds(pl.multiple_of((1 - ylo) * YR, YR), YR)
    own_rows = pl.ds(pl.multiple_of(ylo * YR, YR), YR)
    scale = 1.0 / persons

    def finish(kind, g):
        _, r = buffers(kind, g)
        p = product(kind, g, 0)
        for way in range(2):
            full_copy(kind, g, way, 3).wait_recv()
        p = p + r[0, 3].astype(F32) + r[1, 3].astype(F32)
        if kind == "diag":
            diag_mine[g] = p
            diag_ys[g] = p.astype(BF16)
        elif kind == "last":
            last_mine[...] = p
            last_ys[...] = last_mine[other_rows, :].astype(BF16)
        else:
            far_mine[g - 3] = p
            far_ys[g - 3] = far_mine[g - 3, other_rows, :].astype(BF16)
        pair_copy(kind, g).start()

    def lanes_of(offset):
        return pl.ds(pl.multiple_of(lax.rem(z + offset, nz) * H, H), H)

    def mirror_copy(i):
        away = (1, 6, 3)[i]
        return pltpu.make_async_remote_copy(
            src_ref=mirror.at[i], dst_ref=mirrored.at[i], send_sem=mir_s.at[i], recv_sem=mir_r.at[i],
            device_id=(snp, lax.rem(samp + 2 * away, nsamp)), device_id_type=MESH,
        )

    def settle(kind, g):
        pair_copy(kind, g).wait()
        if kind == "diag":
            diag_mine[g] = (diag_mine[g] + diag_yg[g].astype(F32)) * scale
            mine = diag_mine[g, own_rows, :]
            out[0, :, lanes_of(6 * g)] = mine[:, :H]
            out[0, :, lanes_of(1 + 2 * g)] = mine[:, H:]
        elif kind == "last":
            out[0, :, lanes_of(4)] = (last_mine[own_rows, :] + last_yg[...].astype(F32)) * scale
        else:
            c = far_chunk(g)
            lanes = pl.ds(pl.multiple_of(lax.rem(c, Q) * W, W), W)
            out[c // Q, :, lanes] = (far_mine[g - 3, own_rows, :] + far_yg[g - 3].astype(F32)) * scale

    def send_mirror(i, g, h):
        turn[...] = diag_mine[g, :, h * H : (h + 1) * H].T
        mirror[i] = turn[own_rows, :]
        mirror_copy(i).start()

    def at_group(g, what):
        @pl.when(jnp.logical_and(g >= 0, g < 2))
        def _():
            what("diag", g)

        @pl.when(g == 2)
        def _():
            what("last", g)

        @pl.when(jnp.logical_and(g >= 3, g < G))
        def _():
            what("far", g)

    def left(kind, g):
        for way in range(2):
            half_copy(kind, g, way).wait_send()
            for t in range(1, 4):
                full_copy(kind, g, way, t).wait_send()

    def stat_left(o, _):
        stat_copy(o).wait_send()
        return 0

    def settled(s):
        at_group(s, settle)

        @pl.when(s == 0)
        def _():
            send_mirror(0, 0, 1)

        @pl.when(s == 1)
        def _():
            send_mirror(1, 1, 0)
            send_mirror(2, 1, 1)

    def body(g, _):
        for q in range(Q):

            @pl.when(jnp.logical_and(odd == 0, g == 3 + q))
            def _():
                sib_copy(q, q).wait_recv()

            @pl.when(jnp.logical_and(odd == 1, g == 3 + 2 * q))
            def _():
                take_ahead(q)

            @pl.when(jnp.logical_and(odd == 1, g == 4 + 2 * q))
            def _():
                sib_copy(q, q).wait_recv()

        for t in range(4):
            at_group(g - t, functools.partial(chain, t=t))
        at_group(g - 4, finish)

        at_group(g - 6, left)

        @pl.when(g >= G)
        def _():
            settled(g - G)

        @pl.when(g == G)
        def _():
            lax.fori_loop(1, nsamp, stat_left, 0)
            ms_copy().wait_send()
            for q in range(Q):
                ahead_copy(q).wait_send()
                sib_copy(q, q).wait_send()

        for q in range(Q):

            @pl.when(jnp.logical_and(odd == 0, g == 2 + 2 * q))
            def _():
                take_ahead(q)

        return 0

    lax.fori_loop(0, G + 4, body, 0)
    for g in range(4, G):
        settle("far", g)
    for i in range(3):
        mirror_copy(i).wait_recv()
        out[0, :, lanes_of((7, 2, 5)[i])] = mirrored[i]

    for g in range(G - 2, G):
        left("far", g)
    for i in range(3):
        mirror_copy(i).wait_send()


def per_device(dosage):
    people, width = dosage.shape
    nsnp, nsamp = lax.axis_size("snp"), lax.axis_size("samp")
    dma = pltpu.SemaphoreType.DMA
    tiles = pl.pallas_call(
        functools.partial(kernel, nsnp, nsamp),
        out_shape=jax.ShapeDtypeStruct((3, YR, width), F32),
        in_specs=[pl.BlockSpec(memory_space=pl.ANY)],
        out_specs=pl.BlockSpec(memory_space=pltpu.VMEM),
        scratch_shapes=[
            pltpu.VMEM((people, width), jnp.int32),
            pltpu.VMEM((Q, people, W), BF16),
            pltpu.VMEM((3 * Q, people, W), BF16),
            pltpu.VMEM((width, people), BF16),
            pltpu.VMEM((24, 128), F32),
            pltpu.VMEM((nsamp, 24, 128), F32),
            pltpu.VMEM((16, 128), F32),
            pltpu.VMEM((16, 128), F32),
            pltpu.VMEM((2 + FAR, 2, 4, H, W), BF16),
            pltpu.VMEM((2 + FAR, 2, 4, H, W), BF16),
            pltpu.VMEM((2, 4, H, H), BF16),
            pltpu.VMEM((2, 4, H, H), BF16),
            pltpu.VMEM((2, H, W), F32),
            pltpu.VMEM((2, H, W), BF16),
            pltpu.VMEM((2, H, W), BF16),
            pltpu.VMEM((H, H), F32),
            pltpu.VMEM((YR, H), BF16),
            pltpu.VMEM((YR, H), BF16),
            pltpu.VMEM((FAR, H, W), F32),
            pltpu.VMEM((FAR, YR, W), BF16),
            pltpu.VMEM((FAR, YR, W), BF16),
            pltpu.VMEM((3, YR, H), F32),
            pltpu.VMEM((3, YR, H), F32),
            pltpu.VMEM((H, H), F32),
            dma((4,)),
            dma((nsamp,)),
            dma((nsamp,)),
            dma,
            dma,
            dma((Q,)),
            dma((Q,)),
            dma((Q,)),
            dma((Q,)),
            dma((G, 2, 4)),
            dma((G, 2, 4)),
            dma((G,)),
            dma((G,)),
            dma((3,)),
            dma((3,)),
        ],
        compiler_params=pltpu.CompilerParams(
            collective_id=0, has_side_effects=True, vmem_limit_bytes=56 * 2**20
        ),
        name="ld_band",
    )(dosage)
    return jnp.transpose(tiles, (1, 0, 2))


def solution(mesh):
    in_specs = (P("samp", "snp"),)
    out_specs = P(("snp", "samp"), None, None)
    return jax.shard_map(
        per_device, mesh=mesh, in_specs=in_specs, out_specs=out_specs, check_vma=False
    )
```

```python
import functools

import jax
import jax.numpy as jnp
from jax import lax
from jax.experimental import pallas as pl
from jax.experimental.pallas import tpu as pltpu
from jax.sharding import PartitionSpec as P

MESH = pl.DeviceIdType.MESH
F32 = jnp.float32
BF16 = jnp.bfloat16

W = 256
Q = 4
H = 128
YR = 64
FAR = 2 * Q
G = 3 + FAR
ODD_ORDER = (8, 4, 9, 5, 10, 6, 11, 7)
EVEN_TAKES = (3, 6, 8, 9)
TURNS = 19


def pick(i, values):
    out = values[0]
    for n in range(1, len(values)):
        out = jnp.where(i == n, values[n], out)
    return out


def kernel(
    nsnp, nsamp, dosage, out,
    held, raw, cols, own_t, stat_own, stat_in, ms_own, ms_in,
    sent, got, last_sent, last_got,
    diag_mine, diag_ys, diag_yg, last_mine, last_ys, last_yg, far_mine, far_ys, far_yg, mirror, mirrored, turn,
    load_sem, stat_s, stat_r, ms_s, ms_r, ahead_s, ahead_r, sib_s, sib_r, sent_s, got_r, ys_s, ys_r, mir_s, mir_r,
):
    people, width = held.shape
    persons = float(people * nsamp)
    snp = lax.axis_index("snp")
    samp = lax.axis_index("samp")
    odd = lax.rem(snp, 2)
    ylo = lax.rem(samp, 2)
    z = samp // 2
    nz = nsamp // 2
    behind = (lax.rem(snp + nsnp - 2, nsnp), samp)
    front = (lax.rem(snp + 2, nsnp), samp)
    sibling = (snp + 1 - 2 * odd, samp)
    pair = (snp, samp + 1 - 2 * ylo)
    ring = ((snp, lax.rem(samp + 2, nsamp)), (snp, lax.rem(samp + nsamp - 2, nsamp)))

    barrier = pltpu.get_barrier_semaphore()
    for d in (behind, front, sibling):
        pl.semaphore_signal(barrier, inc=1, device_id=d, device_id_type=MESH)

    def greet(o, _):
        pl.semaphore_signal(
            barrier, inc=1, device_id=(snp, lax.rem(samp + o, nsamp)), device_id_type=MESH
        )
        return 0

    lax.fori_loop(1, nsamp, greet, 0)

    parts = 4
    step = people // parts

    def load(i):
        rows = pl.ds(i * step, step)
        return pltpu.make_async_copy(dosage.at[rows], held.at[rows], load_sem.at[i])

    for i in range(parts):
        load(i).start()

    def slab(i, acc):
        s1, s2, sm = acc
        x = held[pl.ds(pl.multiple_of(i * 16, 16), 16), :].astype(F32)
        xb = x.astype(BF16)
        for q in range(Q):
            raw[q, pl.ds(pl.multiple_of(i * 16, 16), 16), :] = xb[:, q * W : (q + 1) * W]
        lo, hi = x[:8], x[8:]
        s1 = s1 + (lo + hi)
        s2 = s2 + (lo * lo + hi * hi)
        sm = sm + (jnp.minimum(lo, 0.0) + jnp.minimum(hi, 0.0))
        return s1, s2, sm

    zero = jnp.zeros((8, width), F32)
    acc = (zero, zero, zero)
    for i in range(parts):
        load(i).wait()
        acc = lax.fori_loop(i * (step // 16), (i + 1) * (step // 16), slab, acc)
    for n, a in enumerate(acc):
        row = jnp.sum(a, axis=0, keepdims=True)
        for b in range(8):
            stat_own[n * 8 + b : n * 8 + b + 1, :] = row[:, b * 128 : (b + 1) * 128]

    pl.semaphore_wait(barrier, nsamp - 1 + 3)

    def stat_copy(o):
        return pltpu.make_async_remote_copy(
            src_ref=stat_own, dst_ref=stat_in.at[samp],
            send_sem=stat_s.at[o], recv_sem=stat_r.at[samp],
            device_id=(snp, lax.rem(samp + o, nsamp)), device_id_type=MESH,
        )

    def stat_start(o, _):
        stat_copy(o).start()
        return 0

    lax.fori_loop(1, nsamp, stat_start, 0)

    def ahead_copy(q):
        return pltpu.make_async_remote_copy(
            src_ref=raw.at[q], dst_ref=cols.at[2 * Q + q],
            send_sem=ahead_s.at[q], recv_sem=ahead_r.at[q],
            device_id=behind, device_id_type=MESH,
        )

    def turn_raw(i, _):
        rows = pl.ds(pl.multiple_of(i * 128, 128), 128)
        for q in range(Q):
            own_t[q * W : (q + 1) * W, rows] = raw[q, rows, :].T
        return 0

    lax.fori_loop(0, people // 128, turn_raw, 0)

    def stat_take(o, acc):
        src = lax.rem(samp + o, nsamp)
        pltpu.make_async_remote_copy(
            src_ref=stat_own, dst_ref=stat_in.at[src],
            send_sem=stat_s.at[o], recv_sem=stat_r.at[src],
            device_id=(snp, src), device_id_type=MESH,
        ).wait_recv()
        return acc + stat_in[src]

    sums = lax.fori_loop(1, nsamp, stat_take, stat_own[...])
    missing = -sums[16:24]
    count = persons - missing
    total = sums[0:8] + missing
    square = sums[8:16] - missing
    safe = jnp.maximum(count, 1.0)
    ci, ti, si = count.astype(jnp.int32), total.astype(jnp.int32), square.astype(jnp.int32)
    spare = (ci * si - ti * ti).astype(F32)
    ms_own[0:8, :] = total / safe
    ms_own[8:16, :] = 1.0 / jnp.sqrt(spare / (safe * safe) + 1e-05)

    def ms_copy():
        return pltpu.make_async_remote_copy(
            src_ref=ms_own, dst_ref=ms_in, send_sem=ms_s, recv_sem=ms_r,
            device_id=behind, device_id_type=MESH,
        )

    ms_copy().start()
    for q in range(Q):
        ahead_copy(q).start()

    def row_of(ref, base, q):
        return jnp.concatenate([ref[base + 2 * q : base + 2 * q + 1, :], ref[base + 2 * q + 1 : base + 2 * q + 2, :]], axis=1)

    def standardise(src, sq, dq, ref, q, keep):
        mean = row_of(ref, 0, q)
        spread = row_of(ref, 8, q) * keep

        def body(i, _):
            rows = pl.ds(pl.multiple_of(i * 128, 128), 128)
            v = src[sq, rows, :].astype(F32)
            cols[dq, rows, :] = jnp.where(v >= 0, (v - mean) * spread, 0.0).astype(BF16)
            return 0

        lax.fori_loop(0, people // 128, body, 0)

    def sib_copy(src_chunk, q):
        return pltpu.make_async_remote_copy(
            src_ref=cols.at[src_chunk], dst_ref=cols.at[Q + q],
            send_sem=sib_s.at[q], recv_sem=sib_r.at[q],
            device_id=sibling, device_id_type=MESH,
        )

    for q in range(Q):
        standardise(raw, q, q, ms_own, q, 1.0)

        @pl.when(odd == 1)
        def _():
            sib_copy(q, q).start()

    def standardise_turned(b, _):
        rows = pl.ds(pl.multiple_of(b * H, H), H)
        mean = jnp.broadcast_to(ms_own[pl.ds(b, 1), :], (H, H)).T
        spread = jnp.broadcast_to(ms_own[pl.ds(8 + b, 1), :], (H, H)).T
        for i in range(people // H):
            lanes = slice(i * H, (i + 1) * H)
            v = own_t[rows, lanes].astype(F32)
            own_t[rows, lanes] = jnp.where(v >= 0, (v - mean) * spread, 0.0).astype(BF16)
        return 0

    lax.fori_loop(0, width // H, standardise_turned, 0)
    keep = jnp.where(snp + 2 < nsnp, 1.0, 0.0)

    def take_ahead(q):
        ahead_copy(q).wait_recv()
        if q == 0:
            ms_copy().wait_recv()
        standardise(cols, 2 * Q + q, 2 * Q + q, ms_in, q, keep)

        @pl.when(odd == 0)
        def _():
            sib_copy(2 * Q + q, q).start()

    def far_chunk(g):
        return jnp.where(odd == 1, pick(g - 3, ODD_ORDER), g + 1)

    def piece(at, offset):
        c = lax.rem(at + offset, nz)
        return cols[c // 2, :, pl.ds(pl.multiple_of(lax.rem(c, 2) * H, H), H)]

    def product(kind, g, distance):
        at = lax.rem(z + nz + distance, nz)
        left = own_t[pl.ds(pl.multiple_of(at * H, H), H), :]

        def dot(right):
            return jnp.dot(left, right, preferred_element_type=F32)

        if kind == "far":
            return dot(cols[far_chunk(g)])
        if kind == "last":
            return dot(piece(at, 4))
        return jnp.concatenate([dot(piece(at, 6 * g)), dot(piece(at, 1 + 2 * g))], axis=1)

    def buffers(kind, g):
        if kind == "last":
            return last_sent, last_got
        slot = g if kind == "diag" else g - 1
        return sent.at[slot], got.at[slot]

    def half_copy(kind, g, way):
        s, r = buffers(kind, g)
        rows = pl.ds(way * YR, YR)
        return pltpu.make_async_remote_copy(
            src_ref=s.at[way, 0, rows], dst_ref=r.at[way, 0, rows],
            send_sem=sent_s.at[g, way, 0], recv_sem=got_r.at[g, way, 0],
            device_id=ring[way], device_id_type=MESH,
        )

    def full_copy(kind, g, way, t):
        s, r = buffers(kind, g)
        return pltpu.make_async_remote_copy(
            src_ref=s.at[way, t], dst_ref=r.at[way, t],
            send_sem=sent_s.at[g, way, t], recv_sem=got_r.at[g, way, t],
            device_id=ring[way], device_id_type=MESH,
        )

    def chain(kind, g, t):
        s, r = buffers(kind, g)
        if t == 0:
            p = product(kind, g, 4).astype(BF16)
            for way in range(2):
                s[way, 0, way * YR : (way + 1) * YR, :] = p[way * YR : (way + 1) * YR]
                half_copy(kind, g, way).start()
            return
        for way in range(2):
            p = product(kind, g, (4 - t) * (1 - 2 * way))
            if t == 1:
                half_copy(kind, g, way).wait_recv()
                for h in range(2):
                    rows = slice(h * YR, (h + 1) * YR)
                    ph = p[rows]
                    if h == way:
                        ph = ph + r[way, 0, rows, :].astype(F32)
                    s[way, 1, rows, :] = ph.astype(BF16)
            else:
                full_copy(kind, g, way, t - 1).wait_recv()
                s[way, t] = (p + r[way, t - 1].astype(F32)).astype(BF16)
            full_copy(kind, g, way, t).start()

    def pair_copy(kind, g):
        if kind == "diag":
            src, dst = diag_ys.at[g], diag_yg.at[g]
        elif kind == "last":
            src, dst = last_ys, last_yg
        else:
            src, dst = far_ys.at[g - 3], far_yg.at[g - 3]
        return pltpu.make_async_remote_copy(
            src_ref=src, dst_ref=dst, send_sem=ys_s.at[g], recv_sem=ys_r.at[g],
            device_id=pair, device_id_type=MESH,
        )

    other_rows = pl.ds(pl.multiple_of((1 - ylo) * YR, YR), YR)
    own_rows = pl.ds(pl.multiple_of(ylo * YR, YR), YR)
    scale = 1.0 / persons

    def finish(kind, g):
        _, r = buffers(kind, g)
        p = product(kind, g, 0)
        for way in range(2):
            full_copy(kind, g, way, 3).wait_recv()
        p = p + r[0, 3].astype(F32) + r[1, 3].astype(F32)
        if kind == "diag":
            diag_mine[g] = p
            diag_ys[g] = p.astype(BF16)
        elif kind == "last":
            last_mine[...] = p
            last_ys[...] = last_mine[other_rows, :].astype(BF16)
        else:
            far_mine[g - 3] = p
            far_ys[g - 3] = far_mine[g - 3, other_rows, :].astype(BF16)
        pair_copy(kind, g).start()

    def lanes_of(offset):
        return pl.ds(pl.multiple_of(lax.rem(z + offset, nz) * H, H), H)

    def mirror_copy(i):
        away = (1, 6, 3)[i]
        return pltpu.make_async_remote_copy(
            src_ref=mirror.at[i], dst_ref=mirrored.at[i], send_sem=mir_s.at[i], recv_sem=mir_r.at[i],
            device_id=(snp, lax.rem(samp + 2 * away, nsamp)), device_id_type=MESH,
        )

    def settle(kind, g):
        pair_copy(kind, g).wait()
        if kind == "diag":
            diag_mine[g] = (diag_mine[g] + diag_yg[g].astype(F32)) * scale
            mine = diag_mine[g, own_rows, :]
            out[0, :, lanes_of(6 * g)] = mine[:, :H]
            out[0, :, lanes_of(1 + 2 * g)] = mine[:, H:]
        elif kind == "last":
            out[0, :, lanes_of(4)] = (last_mine[own_rows, :] + last_yg[...].astype(F32)) * scale
        else:
            c = far_chunk(g)
            lanes = pl.ds(pl.multiple_of(lax.rem(c, Q) * W, W), W)
            out[c // Q, :, lanes] = (far_mine[g - 3, own_rows, :] + far_yg[g - 3].astype(F32)) * scale

    def send_mirror(i, g, h):
        turn[...] = diag_mine[g, :, h * H : (h + 1) * H].T
        mirror[i] = turn[own_rows, :]
        mirror_copy(i).start()

    def at_group(g, what):
        @pl.when(jnp.logical_and(g >= 0, g < 2))
        def _():
            what("diag", g)

        @pl.when(g == 2)
        def _():
            what("last", g)

        @pl.when(jnp.logical_and(g >= 3, g < G))
        def _():
            what("far", g)

    def group_at(turn):
        late = jnp.maximum(turn - 3, 0)
        paused = jnp.where(lax.rem(late, 3) == 0, -1, 2 + 2 * (late // 3) + lax.rem(late, 3))
        return jnp.where(jnp.logical_and(odd == 1, turn >= 3), paused, turn)

    def left(kind, g):
        for way in range(2):
            half_copy(kind, g, way).wait_send()
            for t in range(1, 4):
                full_copy(kind, g, way, t).wait_send()

    def stat_left(o, _):
        stat_copy(o).wait_send()
        return 0

    def settled(s):
        at_group(s, settle)

        @pl.when(s == 0)
        def _():
            send_mirror(0, 0, 1)

        @pl.when(s == 1)
        def _():
            send_mirror(1, 1, 0)
            send_mirror(2, 1, 1)

    def body(g, _):
        for q in range(Q):

            @pl.when(jnp.logical_and(odd == 0, g == 3 + q))
            def _():
                sib_copy(q, q).wait_recv()

            @pl.when(jnp.logical_and(odd == 1, g == 4 + 3 * q))
            def _():
                take_ahead(q)

            @pl.when(jnp.logical_and(odd == 1, g == 5 + 3 * q))
            def _():
                sib_copy(q, q).wait_recv()

        for t in range(4):
            at_group(group_at(g - t), functools.partial(chain, t=t))
        at_group(group_at(g - 4), finish)

        at_group(group_at(g - 6), left)

        first = 2 * (g - 11 - 4 * odd)

        @pl.when(jnp.logical_and(first >= 0, first < 8))
        def _():
            settled(first)
            settled(first + 1)

        @pl.when(g == 15)
        def _():
            lax.fori_loop(1, nsamp, stat_left, 0)
            ms_copy().wait_send()
            for q in range(Q):
                ahead_copy(q).wait_send()
                sib_copy(q, q).wait_send()

        for q in range(Q):

            @pl.when(jnp.logical_and(odd == 0, g == EVEN_TAKES[q]))
            def _():
                take_ahead(q)

        return 0

    lax.fori_loop(0, TURNS, body, 0)
    for g in range(8, G):
        settle("far", g)
    for i in range(3):
        mirror_copy(i).wait_recv()
        out[0, :, lanes_of((7, 2, 5)[i])] = mirrored[i]

    @pl.when(odd == 1)
    def _():
        for g in range(G - 2, G):
            left("far", g)

    for i in range(3):
        mirror_copy(i).wait_send()


def per_device(dosage):
    people, width = dosage.shape
    nsnp, nsamp = lax.axis_size("snp"), lax.axis_size("samp")
    dma = pltpu.SemaphoreType.DMA
    tiles = pl.pallas_call(
        functools.partial(kernel, nsnp, nsamp),
        out_shape=jax.ShapeDtypeStruct((3, YR, width), F32),
        in_specs=[pl.BlockSpec(memory_space=pl.ANY)],
        out_specs=pl.BlockSpec(memory_space=pltpu.VMEM),
        scratch_shapes=[
            pltpu.VMEM((people, width), jnp.int32),
            pltpu.VMEM((Q, people, W), BF16),
            pltpu.VMEM((3 * Q, people, W), BF16),
            pltpu.VMEM((width, people), BF16),
            pltpu.VMEM((24, 128), F32),
            pltpu.VMEM((nsamp, 24, 128), F32),
            pltpu.VMEM((16, 128), F32),
            pltpu.VMEM((16, 128), F32),
            pltpu.VMEM((2 + FAR, 2, 4, H, W), BF16),
            pltpu.VMEM((2 + FAR, 2, 4, H, W), BF16),
            pltpu.VMEM((2, 4, H, H), BF16),
            pltpu.VMEM((2, 4, H, H), BF16),
            pltpu.VMEM((2, H, W), F32),
            pltpu.VMEM((2, H, W), BF16),
            pltpu.VMEM((2, H, W), BF16),
            pltpu.VMEM((H, H), F32),
            pltpu.VMEM((YR, H), BF16),
            pltpu.VMEM((YR, H), BF16),
            pltpu.VMEM((FAR, H, W), F32),
            pltpu.VMEM((FAR, YR, W), BF16),
            pltpu.VMEM((FAR, YR, W), BF16),
            pltpu.VMEM((3, YR, H), F32),
            pltpu.VMEM((3, YR, H), F32),
            pltpu.VMEM((H, H), F32),
            dma((4,)),
            dma((nsamp,)),
            dma((nsamp,)),
            dma,
            dma,
            dma((Q,)),
            dma((Q,)),
            dma((Q,)),
            dma((Q,)),
            dma((G, 2, 4)),
            dma((G, 2, 4)),
            dma((G,)),
            dma((G,)),
            dma((3,)),
            dma((3,)),
        ],
        compiler_params=pltpu.CompilerParams(
            collective_id=0, has_side_effects=True, vmem_limit_bytes=56 * 2**20
        ),
        name="ld_band",
    )(dosage)
    return jnp.transpose(tiles, (1, 0, 2))


def solution(mesh):
    in_specs = (P("samp", "snp"),)
    out_specs = P(("snp", "samp"), None, None)
    return jax.shard_map(
        per_device, mesh=mesh, in_specs=in_specs, out_specs=out_specs, check_vma=False
    )
```

```python
import functools

import jax
import jax.numpy as jnp
from jax import lax
from jax.experimental import pallas as pl
from jax.experimental.pallas import tpu as pltpu
from jax.sharding import PartitionSpec as P

MESH = pl.DeviceIdType.MESH
F32 = jnp.float32
BF16 = jnp.bfloat16

W = 256
Q = 4
H = 128
YR = 64
FAR = 2 * Q
G = 3 + FAR
ODD_ORDER = (8, 4, 9, 5, 10, 6, 11, 7)
EVEN_TAKES = (3, 6, 8, 9)
TURNS = 19


def pick(i, values):
    out = values[0]
    for n in range(1, len(values)):
        out = jnp.where(i == n, values[n], out)
    return out


def kernel(
    nsnp, nsamp, dosage, out,
    held, raw, cols, own_t, stat_own, stat_in, ms_own, ms_in,
    sent, got, last_sent, last_got,
    diag_mine, diag_ys, diag_yg, last_mine, last_ys, last_yg, far_mine, far_ys, far_yg, mirror, mirrored, turn,
    load_sem, stat_s, stat_r, ms_s, ms_r, ahead_s, ahead_r, sib_s, sib_r, sent_s, got_r, ys_s, ys_r, mir_s, mir_r,
):
    people, width = held.shape
    persons = float(people * nsamp)
    snp = lax.axis_index("snp")
    samp = lax.axis_index("samp")
    odd = lax.rem(snp, 2)
    ylo = lax.rem(samp, 2)
    z = samp // 2
    nz = nsamp // 2
    behind = (lax.rem(snp + nsnp - 2, nsnp), samp)
    front = (lax.rem(snp + 2, nsnp), samp)
    sibling = (snp + 1 - 2 * odd, samp)
    pair = (snp, samp + 1 - 2 * ylo)
    ring = ((snp, lax.rem(samp + 2, nsamp)), (snp, lax.rem(samp + nsamp - 2, nsamp)))

    barrier = pltpu.get_barrier_semaphore()
    for d in (behind, front, sibling):
        pl.semaphore_signal(barrier, inc=1, device_id=d, device_id_type=MESH)

    def greet(o, _):
        pl.semaphore_signal(
            barrier, inc=1, device_id=(snp, lax.rem(samp + o, nsamp)), device_id_type=MESH
        )
        return 0

    lax.fori_loop(1, nsamp, greet, 0)

    parts = 4
    step = people // parts

    def load(i):
        rows = pl.ds(i * step, step)
        return pltpu.make_async_copy(dosage.at[rows], held.at[rows], load_sem.at[i])

    for i in range(parts):
        load(i).start()

    def slab(i, acc):
        s1, s2, sm = acc
        x = held[pl.ds(pl.multiple_of(i * 16, 16), 16), :].astype(F32)
        xb = x.astype(BF16)
        for q in range(Q):
            raw[q, pl.ds(pl.multiple_of(i * 16, 16), 16), :] = xb[:, q * W : (q + 1) * W]
        lo, hi = x[:8], x[8:]
        s1 = s1 + (lo + hi)
        s2 = s2 + (lo * lo + hi * hi)
        sm = sm + (jnp.minimum(lo, 0.0) + jnp.minimum(hi, 0.0))
        return s1, s2, sm

    zero = jnp.zeros((8, width), F32)
    acc = (zero, zero, zero)
    for i in range(parts):
        load(i).wait()
        acc = lax.fori_loop(i * (step // 16), (i + 1) * (step // 16), slab, acc)
    for n, a in enumerate(acc):
        row = jnp.sum(a, axis=0, keepdims=True)
        for b in range(8):
            stat_own[n * 8 + b : n * 8 + b + 1, :] = row[:, b * 128 : (b + 1) * 128]

    pl.semaphore_wait(barrier, nsamp - 1 + 3)

    def stat_copy(o):
        return pltpu.make_async_remote_copy(
            src_ref=stat_own, dst_ref=stat_in.at[samp],
            send_sem=stat_s.at[o], recv_sem=stat_r.at[samp],
            device_id=(snp, lax.rem(samp + o, nsamp)), device_id_type=MESH,
        )

    def stat_start(o, _):
        stat_copy(o).start()
        return 0

    lax.fori_loop(1, nsamp, stat_start, 0)

    def ahead_copy(q):
        return pltpu.make_async_remote_copy(
            src_ref=raw.at[q], dst_ref=cols.at[2 * Q + q],
            send_sem=ahead_s.at[q], recv_sem=ahead_r.at[q],
            device_id=behind, device_id_type=MESH,
        )

    def turn_raw(i, _):
        rows = pl.ds(pl.multiple_of(i * 128, 128), 128)
        for q in range(Q):
            own_t[q * W : (q + 1) * W, rows] = raw[q, rows, :].T
        return 0

    lax.fori_loop(0, people // 256, turn_raw, 0)

    def stat_take(o, acc):
        src = lax.rem(samp + o, nsamp)
        pltpu.make_async_remote_copy(
            src_ref=stat_own, dst_ref=stat_in.at[src],
            send_sem=stat_s.at[o], recv_sem=stat_r.at[src],
            device_id=(snp, src), device_id_type=MESH,
        ).wait_recv()
        return acc + stat_in[src]

    sums = lax.fori_loop(1, nsamp, stat_take, stat_own[...])
    missing = -sums[16:24]
    count = persons - missing
    total = sums[0:8] + missing
    square = sums[8:16] - missing
    safe = jnp.maximum(count, 1.0)
    ci, ti, si = count.astype(jnp.int32), total.astype(jnp.int32), square.astype(jnp.int32)
    spare = (ci * si - ti * ti).astype(F32)
    ms_own[0:8, :] = total / safe
    ms_own[8:16, :] = 1.0 / jnp.sqrt(spare / (safe * safe) + 1e-05)

    def ms_copy():
        return pltpu.make_async_remote_copy(
            src_ref=ms_own, dst_ref=ms_in, send_sem=ms_s, recv_sem=ms_r,
            device_id=behind, device_id_type=MESH,
        )

    ms_copy().start()
    for q in range(Q):
        ahead_copy(q).start()
    lax.fori_loop(people // 256, people // 128, turn_raw, 0)

    def row_of(ref, base, q):
        return jnp.concatenate([ref[base + 2 * q : base + 2 * q + 1, :], ref[base + 2 * q + 1 : base + 2 * q + 2, :]], axis=1)

    def standardise(src, sq, dq, ref, q, keep):
        mean = row_of(ref, 0, q)
        spread = row_of(ref, 8, q) * keep

        def body(i, _):
            rows = pl.ds(pl.multiple_of(i * 128, 128), 128)
            v = src[sq, rows, :].astype(F32)
            cols[dq, rows, :] = jnp.where(v >= 0, (v - mean) * spread, 0.0).astype(BF16)
            return 0

        lax.fori_loop(0, people // 128, body, 0)

    def sib_copy(src_chunk, q):
        return pltpu.make_async_remote_copy(
            src_ref=cols.at[src_chunk], dst_ref=cols.at[Q + q],
            send_sem=sib_s.at[q], recv_sem=sib_r.at[q],
            device_id=sibling, device_id_type=MESH,
        )

    for q in range(Q):
        standardise(raw, q, q, ms_own, q, 1.0)

        @pl.when(odd == 1)
        def _():
            sib_copy(q, q).start()

    def standardise_turned(b, _):
        rows = pl.ds(pl.multiple_of(b * H, H), H)
        mean = jnp.broadcast_to(ms_own[pl.ds(b, 1), :], (H, H)).T
        spread = jnp.broadcast_to(ms_own[pl.ds(8 + b, 1), :], (H, H)).T
        for i in range(people // H):
            lanes = slice(i * H, (i + 1) * H)
            v = own_t[rows, lanes].astype(F32)
            own_t[rows, lanes] = jnp.where(v >= 0, (v - mean) * spread, 0.0).astype(BF16)
        return 0

    lax.fori_loop(0, width // H, standardise_turned, 0)
    keep = jnp.where(snp + 2 < nsnp, 1.0, 0.0)

    def take_ahead(q):
        ahead_copy(q).wait_recv()
        if q == 0:
            ms_copy().wait_recv()
        standardise(cols, 2 * Q + q, 2 * Q + q, ms_in, q, keep)

        @pl.when(odd == 0)
        def _():
            sib_copy(2 * Q + q, q).start()

    def far_chunk(g):
        return jnp.where(odd == 1, pick(g - 3, ODD_ORDER), g + 1)

    def piece(at, offset):
        c = lax.rem(at + offset, nz)
        return cols[c // 2, :, pl.ds(pl.multiple_of(lax.rem(c, 2) * H, H), H)]

    def product(kind, g, distance):
        at = lax.rem(z + nz + distance, nz)
        left = own_t[pl.ds(pl.multiple_of(at * H, H), H), :]

        def dot(right):
            return jnp.dot(left, right, preferred_element_type=F32)

        if kind == "far":
            return dot(cols[far_chunk(g)])
        if kind == "last":
            return dot(piece(at, 4))
        return jnp.concatenate([dot(piece(at, 6 * g)), dot(piece(at, 1 + 2 * g))], axis=1)

    def buffers(kind, g):
        if kind == "last":
            return last_sent, last_got
        slot = g if kind == "diag" else g - 1
        return sent.at[slot], got.at[slot]

    def half_copy(kind, g, way):
        s, r = buffers(kind, g)
        rows = pl.ds(way * YR, YR)
        return pltpu.make_async_remote_copy(
            src_ref=s.at[way, 0, rows], dst_ref=r.at[way, 0, rows],
            send_sem=sent_s.at[g, way, 0], recv_sem=got_r.at[g, way, 0],
            device_id=ring[way], device_id_type=MESH,
        )

    def full_copy(kind, g, way, t):
        s, r = buffers(kind, g)
        return pltpu.make_async_remote_copy(
            src_ref=s.at[way, t], dst_ref=r.at[way, t],
            send_sem=sent_s.at[g, way, t], recv_sem=got_r.at[g, way, t],
            device_id=ring[way], device_id_type=MESH,
        )

    def chain(kind, g, t):
        s, r = buffers(kind, g)
        if t == 0:
            p = product(kind, g, 4).astype(BF16)
            for way in range(2):
                s[way, 0, way * YR : (way + 1) * YR, :] = p[way * YR : (way + 1) * YR]
                half_copy(kind, g, way).start()
            return
        for way in range(2):
            p = product(kind, g, (4 - t) * (1 - 2 * way))
            if t == 1:
                half_copy(kind, g, way).wait_recv()
                for h in range(2):
                    rows = slice(h * YR, (h + 1) * YR)
                    ph = p[rows]
                    if h == way:
                        ph = ph + r[way, 0, rows, :].astype(F32)
                    s[way, 1, rows, :] = ph.astype(BF16)
            else:
                full_copy(kind, g, way, t - 1).wait_recv()
                s[way, t] = (p + r[way, t - 1].astype(F32)).astype(BF16)
            full_copy(kind, g, way, t).start()

    def pair_copy(kind, g):
        if kind == "diag":
            src, dst = diag_ys.at[g], diag_yg.at[g]
        elif kind == "last":
            src, dst = last_ys, last_yg
        else:
            src, dst = far_ys.at[g - 3], far_yg.at[g - 3]
        return pltpu.make_async_remote_copy(
            src_ref=src, dst_ref=dst, send_sem=ys_s.at[g], recv_sem=ys_r.at[g],
            device_id=pair, device_id_type=MESH,
        )

    other_rows = pl.ds(pl.multiple_of((1 - ylo) * YR, YR), YR)
    own_rows = pl.ds(pl.multiple_of(ylo * YR, YR), YR)
    scale = 1.0 / persons

    def finish(kind, g):
        _, r = buffers(kind, g)
        p = product(kind, g, 0)
        for way in range(2):
            full_copy(kind, g, way, 3).wait_recv()
        p = p + r[0, 3].astype(F32) + r[1, 3].astype(F32)
        if kind == "diag":
            diag_mine[g] = p
            diag_ys[g] = p.astype(BF16)
        elif kind == "last":
            last_mine[...] = p
            last_ys[...] = last_mine[other_rows, :].astype(BF16)
        else:
            far_mine[g - 3] = p
            far_ys[g - 3] = far_mine[g - 3, other_rows, :].astype(BF16)
        pair_copy(kind, g).start()

    def lanes_of(offset):
        return pl.ds(pl.multiple_of(lax.rem(z + offset, nz) * H, H), H)

    def mirror_copy(i):
        away = (1, 6, 3)[i]
        return pltpu.make_async_remote_copy(
            src_ref=mirror.at[i], dst_ref=mirrored.at[i], send_sem=mir_s.at[i], recv_sem=mir_r.at[i],
            device_id=(snp, lax.rem(samp + 2 * away, nsamp)), device_id_type=MESH,
        )

    def settle(kind, g):
        pair_copy(kind, g).wait()
        if kind == "diag":
            diag_mine[g] = (diag_mine[g] + diag_yg[g].astype(F32)) * scale
            mine = diag_mine[g, own_rows, :]
            out[0, :, lanes_of(6 * g)] = mine[:, :H]
            out[0, :, lanes_of(1 + 2 * g)] = mine[:, H:]
        elif kind == "last":
            out[0, :, lanes_of(4)] = (last_mine[own_rows, :] + last_yg[...].astype(F32)) * scale
        else:
            c = far_chunk(g)
            lanes = pl.ds(pl.multiple_of(lax.rem(c, Q) * W, W), W)
            out[c // Q, :, lanes] = (far_mine[g - 3, own_rows, :] + far_yg[g - 3].astype(F32)) * scale

    def send_mirror(i, g, h):
        turn[...] = diag_mine[g, :, h * H : (h + 1) * H].T
        mirror[i] = turn[own_rows, :]
        mirror_copy(i).start()

    def at_group(g, what):
        @pl.when(jnp.logical_and(g >= 0, g < 2))
        def _():
            what("diag", g)

        @pl.when(g == 2)
        def _():
            what("last", g)

        @pl.when(jnp.logical_and(g >= 3, g < G))
        def _():
            what("far", g)

    def group_at(turn):
        late = jnp.maximum(turn - 3, 0)
        paused = jnp.where(lax.rem(late, 3) == 0, -1, 2 + 2 * (late // 3) + lax.rem(late, 3))
        return jnp.where(jnp.logical_and(odd == 1, turn >= 3), paused, turn)

    def left(kind, g):
        for way in range(2):
            half_copy(kind, g, way).wait_send()
            for t in range(1, 4):
                full_copy(kind, g, way, t).wait_send()

    def stat_left(o, _):
        stat_copy(o).wait_send()
        return 0

    def settled(s):
        at_group(s, settle)

        @pl.when(s == 0)
        def _():
            send_mirror(0, 0, 1)

        @pl.when(s == 1)
        def _():
            send_mirror(1, 1, 0)
            send_mirror(2, 1, 1)

    def body(g, _):
        for q in range(Q):

            @pl.when(jnp.logical_and(odd == 0, g == 3 + q))
            def _():
                sib_copy(q, q).wait_recv()

            @pl.when(jnp.logical_and(odd == 1, g == 4 + 3 * q))
            def _():
                take_ahead(q)

            @pl.when(jnp.logical_and(odd == 1, g == 5 + 3 * q))
            def _():
                sib_copy(q, q).wait_recv()

        for t in range(4):
            at_group(group_at(g - t), functools.partial(chain, t=t))
        at_group(group_at(g - 4), finish)

        at_group(group_at(g - 6), left)

        first = 2 * (g - 11 - 4 * odd)

        @pl.when(jnp.logical_and(first >= 0, first < 8))
        def _():
            settled(first)
            settled(first + 1)

        @pl.when(g == 15)
        def _():
            lax.fori_loop(1, nsamp, stat_left, 0)
            ms_copy().wait_send()
            for q in range(Q):
                ahead_copy(q).wait_send()
                sib_copy(q, q).wait_send()

        for q in range(Q):

            @pl.when(jnp.logical_and(odd == 0, g == EVEN_TAKES[q]))
            def _():
                take_ahead(q)

        return 0

    lax.fori_loop(0, TURNS, body, 0)
    for g in range(8, G):
        settle("far", g)
    for i in range(3):
        mirror_copy(i).wait_recv()
        out[0, :, lanes_of((7, 2, 5)[i])] = mirrored[i]

    @pl.when(odd == 1)
    def _():
        for g in range(G - 2, G):
            left("far", g)

    for i in range(3):
        mirror_copy(i).wait_send()


def per_device(dosage):
    people, width = dosage.shape
    nsnp, nsamp = lax.axis_size("snp"), lax.axis_size("samp")
    dma = pltpu.SemaphoreType.DMA
    tiles = pl.pallas_call(
        functools.partial(kernel, nsnp, nsamp),
        out_shape=jax.ShapeDtypeStruct((3, YR, width), F32),
        in_specs=[pl.BlockSpec(memory_space=pl.ANY)],
        out_specs=pl.BlockSpec(memory_space=pltpu.VMEM),
        scratch_shapes=[
            pltpu.VMEM((people, width), jnp.int32),
            pltpu.VMEM((Q, people, W), BF16),
            pltpu.VMEM((3 * Q, people, W), BF16),
            pltpu.VMEM((width, people), BF16),
            pltpu.VMEM((24, 128), F32),
            pltpu.VMEM((nsamp, 24, 128), F32),
            pltpu.VMEM((16, 128), F32),
            pltpu.VMEM((16, 128), F32),
            pltpu.VMEM((2 + FAR, 2, 4, H, W), BF16),
            pltpu.VMEM((2 + FAR, 2, 4, H, W), BF16),
            pltpu.VMEM((2, 4, H, H), BF16),
            pltpu.VMEM((2, 4, H, H), BF16),
            pltpu.VMEM((2, H, W), F32),
            pltpu.VMEM((2, H, W), BF16),
            pltpu.VMEM((2, H, W), BF16),
            pltpu.VMEM((H, H), F32),
            pltpu.VMEM((YR, H), BF16),
            pltpu.VMEM((YR, H), BF16),
            pltpu.VMEM((FAR, H, W), F32),
            pltpu.VMEM((FAR, YR, W), BF16),
            pltpu.VMEM((FAR, YR, W), BF16),
            pltpu.VMEM((3, YR, H), F32),
            pltpu.VMEM((3, YR, H), F32),
            pltpu.VMEM((H, H), F32),
            dma((4,)),
            dma((nsamp,)),
            dma((nsamp,)),
            dma,
            dma,
            dma((Q,)),
            dma((Q,)),
            dma((Q,)),
            dma((Q,)),
            dma((G, 2, 4)),
            dma((G, 2, 4)),
            dma((G,)),
            dma((G,)),
            dma((3,)),
            dma((3,)),
        ],
        compiler_params=pltpu.CompilerParams(
            collective_id=0, has_side_effects=True, vmem_limit_bytes=56 * 2**20
        ),
        name="ld_band",
    )(dosage)
    return jnp.transpose(tiles, (1, 0, 2))


def solution(mesh):
    in_specs = (P("samp", "snp"),)
    out_specs = P(("snp", "samp"), None, None)
    return jax.shard_map(
        per_device, mesh=mesh, in_specs=in_specs, out_specs=out_specs, check_vma=False
    )
```
